512 devices in a mesh: user: 64 (over z, y), item: 8 (over x, core).
Axes of the slice: x: 4, y: 4, z: 16, core: 2. Of those that a mesh axis runs over, the one named last changes fastest.
Arguments:
- candidates: bfloat16 [1024, 128, 512], P(('user', 'item')), may hold values from -6 to 6
- proj_weight: bfloat16 [512, 2048], P('user'), may hold values from -0.25 to 0.25
- out_weight: bfloat16 [512, 512], P('user'), may hold values from -0.25 to 0.25
- history_kv: bfloat16 [1024, 4, 64, 1024], P('item', None, 'user'), may hold values from -6 to 6
- scorer_user: int32 [1024], replicated, may hold values from 0 to 1023, as said below
- hist_len: int32 [1024], P(('user', 'item')), may hold values from 16 to 256, as said below
- cand_item: int32 [1024, 128], P(('user', 'item')), may hold values from 0 to 8191, as said below
- item_table: bfloat16 [8192, 512], P('item'), may hold values from -0.25 to 0.25
Outputs:
- logits: float32 [1024, 128], P(('user', 'item'))
The draws below stay inside these ranges and needn't reach their ends.
Inputs may be any that keep to these rules, and one draw needn't show every extreme that they name: `scorer_user`: A permutation of all users; scorer slot s lies on the device at position s // 2 of the flattened user, item axes, and its user lies in owner block (s // 2) % 8 of 128 users. `hist_len`: some slot has length 256. `cand_item`: item id // 1024 is the item shard holding its row. In the rows of one device no shard is named by more than 96 rows, and in every draw one shard is named by exactly 96 rows of every device.
All inputs are finite; a program needn't handle non-finite values.
Results may differ from the reference program's by a relative error of at most 0.0075.
Values may be sent and summed in bfloat16 or wider, within the bound.
No kernel may reach another device: no remote copies, remote signals or barrier semaphores. Data moves between devices by JAX's collectives and lax.ppermute only.
A program may use at most 64 MiB of HBM per device.

```python
import jax
import jax.numpy as jnp
from jax import lax

D = 512
HEADS = 4
DH = 128
U_DEV = 2
CAND = 128
HIST_DEV = 4
ITEM_ROWS = 1024
OWNERS = 64
ITEM_SHARDS = 8
HIST = 256
USERS = 1024
GROUP_USERS = 128
ITEMS = 8192
CAP = 96


def draw_scorer_user(key, part):
    key = jax.random.fold_in(key, 11)
    group_keys = jax.random.split(key, ITEM_SHARDS)
    shuffles = jax.vmap(lambda one_key: jax.random.permutation(one_key, GROUP_USERS))(group_keys)
    slot_index = jnp.arange(USERS, dtype=jnp.int32)
    device_index = slot_index // U_DEV
    group_index = device_index % ITEM_SHARDS
    local_index = device_index // ITEM_SHARDS * U_DEV + slot_index % U_DEV
    return (group_index * GROUP_USERS + shuffles[group_index, local_index]).astype(jnp.int32)


def draw_hist_len(key, part):
    key = jax.random.fold_in(key, 12)
    lengths = jax.random.randint(key, (USERS,), HIST // 16, HIST + 1)
    lengths = jnp.where(jnp.arange(USERS) == 0, HIST, lengths)
    return lengths.astype(jnp.int32)


def draw_cand_item(key, part):
    key = jax.random.fold_in(key, 13)
    hot_key, order_key, row_key = jax.random.split(key, 3)
    rows_dev = U_DEV * CAND
    block_count = USERS // U_DEV
    hot_shard = jax.random.randint(hot_key, (), 0, ITEM_SHARDS)
    order_keys = jax.random.split(order_key, block_count)
    slot_rank = jax.vmap(lambda one_key: jax.random.permutation(one_key, rows_dev))(order_keys)
    other = (slot_rank - CAP) * (ITEM_SHARDS - 1) // (rows_dev - CAP)
    other = other + (other >= hot_shard).astype(jnp.int32)
    item_shard = jnp.where(slot_rank < CAP, hot_shard, other)
    table_row = jax.random.randint(row_key, (block_count, rows_dev), 0, ITEM_ROWS)
    item_ids = item_shard * ITEM_ROWS + table_row
    return item_ids.reshape(USERS, CAND).astype(jnp.int32)


def steps_of(rng, shape, cuts, least, largest):
    level = 1.0
    for axis_at, shards_of in cuts:
        heights = jax.random.uniform(jax.random.fold_in(jax.random.fold_in(rng, 6), axis_at), (shards_of,), jnp.float32, least / len(cuts), largest / len(cuts))
        level = level * jnp.repeat(jnp.exp(heights), shape[axis_at] // shards_of).reshape((-1,) + (1,) * (len(shape) - 1 - axis_at))
    return level


def normal_values(rng, extent, scale, most, shards=(), held_as=jnp.bfloat16):
    array = scale * jax.random.normal(rng, extent, jnp.float32)
    if shards:
        array = array * steps_of(rng, extent, shards, -0.22, 0.18)
    return jnp.clip(array, -most, most).astype(held_as)


def setup_inputs(seed: int = 0) -> dict:
    key_of = jax.random.split(jax.random.key(seed), 9)
    candidates = normal_values(key_of[0], (USERS, CAND, D), 1.0, 6.0, ((0, 512),))
    proj_weight = normal_values(key_of[1], (D, 4 * D), D ** -0.5, 0.25, ((0, 64),))
    out_weight = normal_values(key_of[2], (D, D), D ** -0.5, 0.25, ((0, 64),))
    history_kv = normal_values(key_of[3], (USERS, HIST_DEV, OWNERS, 2 * D), 1.0, 6.0, ((0, 8), (2, 64)))
    scorer_user = draw_scorer_user(jax.random.fold_in(key_of[8], 71), 0)
    hist_len = draw_hist_len(jax.random.fold_in(key_of[8], 71), 0)
    cand_item = draw_cand_item(jax.random.fold_in(key_of[8], 71), 0)
    item_table = normal_values(key_of[7], (ITEMS, D), D ** -0.5, 0.25, ((0, 8),))
    return {"candidates": candidates, "proj_weight": proj_weight, "out_weight": out_weight, "history_kv": history_kv, "scorer_user": scorer_user, "hist_len": hist_len, "cand_item": cand_item, "item_table": item_table}


def layer_norm(values):
    center = values - lax.optimization_barrier(jnp.mean(values, axis=-1, keepdims=True))
    spread = lax.optimization_barrier(jnp.mean(center * center, axis=-1, keepdims=True))
    return center * lax.rsqrt(spread + 1e-06)

def score_block(block_args, proj_weight, out_weight, history, item_table):
    cand_block, owner_ids, lengths, item_ids = block_args
    block_users = cand_block.shape[0]
    row_count = block_users * CAND
    cand_rows = cand_block.reshape(row_count, D)
    normed = layer_norm(cand_rows.astype(jnp.float32)).astype(jnp.bfloat16)
    proj = jax.nn.silu(jnp.dot(normed, proj_weight, preferred_element_type=jnp.float32))
    gate_u = proj[:, :D]
    cand_v = proj[:, D:2 * D].astype(jnp.bfloat16).reshape(block_users, CAND, HEADS, DH)
    cand_q = proj[:, 2 * D:3 * D].astype(jnp.bfloat16).reshape(block_users, CAND, HEADS, DH)
    cand_k = proj[:, 3 * D:].astype(jnp.bfloat16).reshape(block_users, CAND, HEADS, DH)
    picked = jnp.take(history, owner_ids, axis=0)
    hist_keys = picked[:, :, :D].reshape(block_users, HIST, HEADS, DH)
    hist_values = picked[:, :, D:].reshape(block_users, HIST, HEADS, DH)
    score_scale = DH ** (-0.5)
    scores = jnp.einsum('uchx,uphx->uhcp', cand_q.astype(jnp.float32), hist_keys.astype(jnp.float32)) * score_scale
    live_mask = jnp.arange(HIST)[None, :] < lengths[:, None]
    hist_w = jnp.where(live_mask[:, None, None, :], jax.nn.silu(scores), 0.0).astype(jnp.bfloat16)
    attention = jnp.einsum('uhcp,uphx->uchx', hist_w.astype(jnp.float32), hist_values.astype(jnp.float32))
    self_score = lax.optimization_barrier(jnp.sum(cand_q.astype(jnp.float32) * cand_k.astype(jnp.float32), axis=-1)) * score_scale
    self_w = jax.nn.silu(self_score).astype(jnp.bfloat16)
    attention = attention + self_w.astype(jnp.float32)[..., None] * cand_v.astype(jnp.float32)
    attended = attention / (lengths.astype(jnp.float32) + 1.0)[:, None, None, None]
    attended = attended.reshape(row_count, D)
    gated = (layer_norm(attended) * gate_u).astype(jnp.bfloat16)
    final = cand_rows.astype(jnp.float32) + jnp.dot(gated, out_weight, preferred_element_type=jnp.float32)
    unit = (final * lax.rsqrt(lax.optimization_barrier(jnp.mean(final * final, axis=-1, keepdims=True)) + 1e-06)).astype(jnp.bfloat16)
    table_rows = jnp.take(item_table, item_ids.reshape(row_count), axis=0)
    logits = lax.optimization_barrier(jnp.sum(unit.astype(jnp.float32) * table_rows.astype(jnp.float32), axis=-1))
    return logits.reshape(block_users, CAND)

def reference(candidates, proj_weight, out_weight, history_kv, scorer_user, hist_len, cand_item, item_table):
    history = history_kv.reshape(USERS, HIST, 2 * D)
    block_users = U_DEV * ITEM_SHARDS
    block_count = USERS // block_users
    block_args = (candidates.reshape(block_count, block_users, CAND, D), scorer_user.reshape(block_count, block_users), hist_len.reshape(block_count, block_users), cand_item.reshape(block_count, block_users, CAND))
    logits = lax.map(lambda args: score_block(args, proj_weight, out_weight, history, item_table), block_args)
    return logits.reshape(USERS, CAND)
```

```python
import functools

import jax
import jax.numpy as jnp
from jax import lax
from jax.experimental import pallas as pl
from jax.experimental.pallas import tpu as pltpu
from jax.sharding import Mesh, PartitionSpec as P

HEADS = 4
CAP = 96
F32 = jnp.float32
BF16 = jnp.bfloat16
VMEM = pltpu.VMEM
SMEM = pltpu.SMEM
VMEM_LIMIT = 40 * 1024 * 1024

USER = ("z", "y")
ITEM = ("x", "core")


def params():
    return pltpu.CompilerParams(vmem_limit_bytes=VMEM_LIMIT)


def silu(values):
    return values * jax.nn.sigmoid(values)


def iota(shape, dim):
    return lax.broadcasted_iota(jnp.int32, shape, dim)


def dot(a, b):
    return jnp.dot(a, b, preferred_element_type=F32)


def spread_kernel(place, proj_weight, out_weight, out):
    item = place[0]
    chosen = iota((proj_weight.shape[0], 1), 0) == item
    wide = jnp.where(chosen, proj_weight[...].astype(F32), 0.0)
    narrow = jnp.where(chosen, out_weight[...].astype(F32), 0.0)
    row = jnp.concatenate(
        [jnp.sum(wide, axis=0, keepdims=True), jnp.sum(narrow, axis=0, keepdims=True)], axis=1
    )
    half = row.shape[1] // 2
    pair = jnp.concatenate([row[:, :half], row[:, half:]], axis=0).astype(BF16)
    for k in range(out.shape[0]):
        out[k] = pair


def spread(place, proj_weight, out_weight, copies):
    columns = proj_weight.shape[1] + out_weight.shape[1]
    return pl.pallas_call(
        spread_kernel,
        out_shape=jax.ShapeDtypeStruct((copies, 2, columns // 2), BF16),
        in_specs=[pl.BlockSpec(memory_space=SMEM)] + [pl.BlockSpec(memory_space=VMEM)] * 2,
        out_specs=pl.BlockSpec(memory_space=VMEM),
        compiler_params=params(),
        name="spread_weight_row",
    )(place, proj_weight, out_weight)


def block_kernel(first, rows, out):
    whole = jnp.concatenate([rows[:, 0, :], rows[:, 1, :]], axis=1)
    peers, width = whole.shape[0], out.shape[1]
    for k in range(whole.shape[1] // width):
        out[k * peers : (k + 1) * peers, :] = whole[:, k * width : (k + 1) * width]


def block(first, rows, width):
    peers, _, half = rows.shape
    return pl.pallas_call(
        block_kernel,
        out_shape=jax.ShapeDtypeStruct((peers * 2 * half // width, width), BF16),
        in_specs=[pl.BlockSpec(memory_space=pl.ANY), pl.BlockSpec(memory_space=VMEM)],
        out_specs=pl.BlockSpec(memory_space=VMEM),
        compiler_params=params(),
        name="block_weight_rows",
    )(first, rows)


def pick_kernel(slots, place, hist, first, out):
    item = place[0]
    owners = out.shape[0]
    users = out.shape[1]
    group = hist.shape[0]

    def one(owner, carry):
        for slot in range(users):
            local = slots[(owner * 8 + item) * users + slot] - item * group
            out[owner, slot] = hist[local]
        return carry

    lax.fori_loop(0, owners, one, 0, unroll=4)


def pick(scorer_user, place, hist, first, owners, users):
    return pl.pallas_call(
        pick_kernel,
        out_shape=jax.ShapeDtypeStruct((owners, users) + hist.shape[1:], hist.dtype),
        in_specs=[
            pl.BlockSpec(memory_space=SMEM),
            pl.BlockSpec(memory_space=SMEM),
            pl.BlockSpec(memory_space=VMEM),
            pl.BlockSpec(memory_space=pl.ANY),
        ],
        out_specs=pl.BlockSpec(memory_space=VMEM),
        compiler_params=params(),
        name="pick_history",
    )(scorer_user, place, hist, first)


def fetch_kernel(place, ids, table, out):
    item = place[0]
    x, core = place[1], place[2]
    rows = table.shape[0]
    count = ids.shape[1]
    before = (iota((count, count), 0) < iota((count, count), 1)).astype(BF16)
    all_ids = ids[...]
    mine = (all_ids // rows == item)
    mine_f = mine.astype(F32)
    rank = dot(mine.astype(BF16), before)
    key = jnp.where(mine, rank, -1.0)
    local = (all_ids % rows).astype(F32)
    tab = table[...]
    peer_of = iota((ids.shape[0], 1), 0)
    for k in range(8):
        peer = ((x + k // 2) % 4) * 2 + (core + k % 2) % 2
        choose = (peer_of == peer).astype(F32)
        key_k = jnp.sum((key + 1.0) * choose, axis=0, keepdims=True) - 1.0
        local_k = jnp.sum(local * choose, axis=0, keepdims=True)
        slot = iota((CAP, count), 0).astype(F32)
        row_of = jnp.sum(jnp.where(slot == key_k, local_k, 0.0), axis=1, keepdims=True)
        hot = (iota((CAP, rows), 1).astype(F32) == row_of).astype(BF16)
        out[k // 2, k % 2] = dot(hot, tab).astype(BF16)


def fetch(place, ids, table):
    return pl.pallas_call(
        fetch_kernel,
        out_shape=jax.ShapeDtypeStruct((4, 2, CAP, table.shape[1]), table.dtype),
        in_specs=[
            pl.BlockSpec(memory_space=SMEM),
            pl.BlockSpec(memory_space=VMEM),
            pl.BlockSpec(memory_space=VMEM),
        ],
        out_specs=pl.BlockSpec(memory_space=VMEM),
        compiler_params=params(),
        name="fetch_rows",
    )(place, ids, table)


def pack_x_kernel(found, weight, *outs):
    for k, out in enumerate(outs):
        out[:CAP] = found[k, 0]
        out[CAP:-CAP] = weight[...]
        out[-CAP:] = found[k, 1]


def pack_x(found, weight):
    rows = weight.shape[0] + 2 * CAP
    return pl.pallas_call(
        pack_x_kernel,
        out_shape=(jax.ShapeDtypeStruct((rows, weight.shape[1]), BF16),) * 4,
        in_specs=[pl.BlockSpec(memory_space=VMEM)] * 2,
        out_specs=(pl.BlockSpec(memory_space=VMEM),) * 4,
        compiler_params=params(),
        name="pack_for_x",
    )(found, weight)


def pack_core_kernel(*refs):
    out = refs[-1]
    for k, ref in enumerate(refs[:-1]):
        out[k] = ref[CAP:]


def pack_core(pieces):
    rows, width = pieces[0].shape
    return pl.pallas_call(
        pack_core_kernel,
        out_shape=jax.ShapeDtypeStruct((4, rows - CAP, width), BF16),
        in_specs=[pl.BlockSpec(memory_space=VMEM)] * 4,
        out_specs=pl.BlockSpec(memory_space=VMEM),
        compiler_params=params(),
        name="pack_for_core",
    )(*pieces)


def proj_kernel(
    place, ids, cand, p0, p1, p2, p3, other, rows_out, gate, query, self_term, out_weight
):
    own = (p0, p1, p2, p3)
    x, core = place[1], place[2]
    rows, width = cand.shape
    values = cand[...].astype(F32)
    center = values - jnp.mean(values, axis=-1, keepdims=True)
    spread = jnp.mean(center * center, axis=-1, keepdims=True)
    normed = (center * lax.rsqrt(spread + 1e-06)).astype(BF16)
    g = iota((width, width), 1)
    from_x = (x + 4 - (g // 64) % 4) % 4
    from_core = (core + g // 256) % 2
    natural = (g % 16) * 32 + ((g // 16) % 4) * 8 + from_x * 2 + from_core
    perm = (iota((width, width), 0) == natural).astype(BF16)
    normed = dot(normed, perm).astype(BF16)

    def weight(cols):
        parts = []
        for y in range(4):
            at = (y * 5 + cols) * 16
            parts.append(at)
        blocks = [own[k][CAP + at : CAP + at + 16] for k in range(4) for at in parts]
        blocks += [other[k, at : at + 16] for k in range(4) for at in parts]
        return jnp.concatenate(blocks, axis=0)

    out_weight[...] = dot(perm, weight(4)).astype(BF16)
    gate[...] = silu(dot(normed, weight(0)))
    value = silu(dot(normed, weight(1))).astype(BF16).astype(F32)
    q = silu(dot(normed, weight(2))).astype(BF16)
    k = silu(dot(normed, weight(3))).astype(BF16)
    query[...] = q
    product = q.astype(F32) * k.astype(F32)
    head = width // HEADS
    for h in range(HEADS):
        cols = slice(h * head, (h + 1) * head)
        score = jnp.sum(product[:, cols], axis=-1, keepdims=True) * head ** (-0.5)
        self_term[:, cols] = silu(score).astype(BF16).astype(F32) * value[:, cols]

    shard = ids[...] // 1024
    before = (iota((rows, rows), 0) < iota((rows, rows), 1)).astype(BF16)
    hot = iota((8, rows), 0) == shard
    ranks = dot(hot.astype(BF16), before)
    rank = jnp.sum(jnp.where(hot, ranks, 0.0), axis=0, keepdims=True)
    offset = ((x + 4 - shard // 2) % 4) * 2 + (core + 2 - shard % 2) % 2
    total = jnp.zeros((rows, width), F32)
    for j in range(8):
        key = jnp.where(offset == j, rank, -1.0)
        chosen = (iota((CAP, rows), 0).astype(F32) == key).astype(BF16)
        piece = other[j // 2, -CAP:] if j % 2 else own[j // 2][:CAP]
        total += lax.dot_general(
            chosen, piece, (((0,), (0,)), ((), ())), preferred_element_type=F32
        )
    rows_out[...] = total.astype(BF16)


def project(place, ids, cand, pieces, other):
    rows, width = cand.shape
    return pl.pallas_call(
        proj_kernel,
        out_shape=(
            jax.ShapeDtypeStruct((rows, width), BF16),
            jax.ShapeDtypeStruct((rows, width), F32),
            jax.ShapeDtypeStruct((rows, width), BF16),
            jax.ShapeDtypeStruct((rows, width), F32),
            jax.ShapeDtypeStruct((width, width), BF16),
        ),
        in_specs=[pl.BlockSpec(memory_space=SMEM)] + [pl.BlockSpec(memory_space=VMEM)] * 7,
        out_specs=(pl.BlockSpec(memory_space=VMEM),) * 5,
        compiler_params=params(),
        name="project",
    )(place, ids, cand, *pieces, other)


def score_kernel(lengths, hist, query, self_term, gate, cand, out_weight, rows_ref, out):
    owners, users, per_owner, _ = hist.shape
    width = cand.shape[1]
    head = width // HEADS
    positions = owners * per_owner
    count = cand.shape[0] // users
    lane = iota((1, positions), 1)
    position = (lane % per_owner) * owners + lane // per_owner
    for user in range(users):
        at = slice(user * count, (user + 1) * count)
        length = lengths[user]
        live = position < length
        kv = hist[:, user].reshape(positions, 2 * width)
        parts = []
        for h in range(HEADS):
            cols = slice(h * head, (h + 1) * head)
            scores = lax.dot_general(
                query[at, cols], kv[:, cols], (((1,), (1,)), ((), ())), preferred_element_type=F32
            ) * (head ** (-0.5))
            weights = jnp.where(live, silu(scores), 0.0).astype(BF16)
            parts.append(dot(weights, kv[:, width + h * head : width + (h + 1) * head]))
        attended = (jnp.concatenate(parts, axis=1) + self_term[at]) / (
            length.astype(F32) + 1.0
        )
        center = attended - jnp.mean(attended, axis=-1, keepdims=True)
        spread = jnp.mean(center * center, axis=-1, keepdims=True)
        gated = (center * lax.rsqrt(spread + 1e-06) * gate[at]).astype(BF16)
        final = cand[at].astype(F32) + dot(gated, out_weight[...])
        scale = lax.rsqrt(jnp.mean(final * final, axis=-1, keepdims=True) + 1e-06)
        unit = (final * scale).astype(BF16).astype(F32)
        logit = jnp.sum(unit * rows_ref[at].astype(F32), axis=-1, keepdims=True)
        eye = iota((count, count), 0) == iota((count, count), 1)
        out[user : user + 1, :] = jnp.sum(jnp.where(eye, logit, 0.0), axis=0, keepdims=True)


def score(lengths, hist, query, self_term, gate, cand, out_weight, rows):
    users = hist.shape[1]
    return pl.pallas_call(
        score_kernel,
        out_shape=jax.ShapeDtypeStruct((users, cand.shape[0] // users), F32),
        in_specs=[pl.BlockSpec(memory_space=SMEM)] + [pl.BlockSpec(memory_space=VMEM)] * 7,
        out_specs=pl.BlockSpec(memory_space=VMEM),
        compiler_params=params(),
        name="score",
    )(lengths, hist, query, self_term, gate, cand, out_weight, rows)


def body(
    candidates, proj_weight, out_weight, history_kv, scorer_user, hist_len, cand_item, item_table
):
    users, count, width = candidates.shape
    cand = candidates.reshape(users * count, width)
    x, core = lax.axis_index("x"), lax.axis_index("core")
    item = x * 2 + core
    place = jnp.stack([item, x, core]).astype(jnp.int32)
    owners = lax.axis_size(USER)

    row = spread(place, proj_weight, out_weight, lax.axis_size("z"))
    rows_z = lax.all_to_all(row, "z", split_axis=0, concat_axis=0, tiled=True)

    my_ids = cand_item.reshape(1, users * count)
    ids = lax.all_gather(my_ids, ITEM, axis=0, tiled=True)
    found = fetch(place, ids, item_table)

    hist = history_kv.reshape(history_kv.shape[0], history_kv.shape[1], -1)
    picked = pick(scorer_user, place, hist, ids, owners, users)
    arrived = lax.all_to_all(picked, USER, split_axis=0, concat_axis=0, tiled=True)

    rows_z = block(picked, rows_z, width)
    rows_zy = lax.all_gather(rows_z, "y", axis=0, tiled=True)
    pieces = list(pack_x(found, rows_zy))
    for k in (1, 3, 2):
        pieces[k] = lax.ppermute(pieces[k], "x", [(j, (j + k) % 4) for j in range(4)])
    other = lax.ppermute(pack_core(pieces), "core", [(0, 1), (1, 0)])
    rows, gate, query, self_term, out_w = project(place, my_ids, cand, pieces, other)
    return score(hist_len, arrived, query, self_term, gate, cand, out_w, rows)


def solution(mesh):
    cut = Mesh(mesh.devices.reshape(16, 4, 4, 2), ("z", "y", "x", "core"))
    return jax.shard_map(
        body,
        mesh=cut,
        in_specs=(
            P(USER + ITEM, None, None),
            P(USER, None),
            P(USER, None),
            P(ITEM, None, USER, None),
            P(),
            P(USER + ITEM),
            P(USER + ITEM, None),
            P(ITEM, None),
        ),
        out_specs=P(USER + ITEM, None),
        check_vma=False,
    )
```

```python
import functools

import jax
import jax.numpy as jnp
from jax import lax
from jax.experimental import pallas as pl
from jax.experimental.pallas import tpu as pltpu
from jax.sharding import Mesh, PartitionSpec as P

HEADS = 4
CAP = 96
F32 = jnp.float32
BF16 = jnp.bfloat16
VMEM = pltpu.VMEM
SMEM = pltpu.SMEM
VMEM_LIMIT = 40 * 1024 * 1024

USER = ("z", "y")
ITEM = ("x", "core")


def params():
    return pltpu.CompilerParams(vmem_limit_bytes=VMEM_LIMIT)


def silu(values):
    return values * jax.nn.sigmoid(values)


def iota(shape, dim):
    return lax.broadcasted_iota(jnp.int32, shape, dim)


def dot(a, b):
    return jnp.dot(a, b, preferred_element_type=F32)


def shard_kernel(proj_weight, out_weight, out):
    width = out.shape[1]
    wide = proj_weight[...].astype(F32)
    parts = [wide[:, k * width : (k + 1) * width] for k in range(4)]
    parts.append(out_weight[...].astype(F32))
    out[...] = jnp.concatenate(parts, axis=0).astype(BF16)


def stack_shard(proj_weight, out_weight):
    rows, width = out_weight.shape
    return pl.pallas_call(
        shard_kernel,
        out_shape=jax.ShapeDtypeStruct((rows * 5, width), BF16),
        in_specs=[pl.BlockSpec(memory_space=VMEM)] * 2,
        out_specs=pl.BlockSpec(memory_space=VMEM),
        compiler_params=params(),
        name="stack_weight_shard",
    )(proj_weight, out_weight)


def block_kernel(p0, p1, my_ids, other_ids, out):
    rows = jnp.concatenate([p0[...].astype(F32), p1[...].astype(F32)], axis=0).astype(BF16)
    count = rows.shape[0]
    k = iota((count, count), 0)
    source = (k % 16) // 8 * (count // 2) + k // 16 * 8 + k % 8
    move = (iota((count, count), 1) == source).astype(BF16)
    ids = jnp.concatenate([my_ids[...], other_ids[...]], axis=0)
    digits = jnp.concatenate([ids // 128, ids % 128], axis=1).astype(F32)
    rest = jnp.zeros((out.shape[0] - count - 2, out.shape[1]), F32)
    out[...] = jnp.concatenate([dot(move, rows), digits, rest], axis=0).astype(BF16)


def block(p0, p1, my_ids, other_ids):
    rows, width = p0.shape
    return pl.pallas_call(
        block_kernel,
        out_shape=jax.ShapeDtypeStruct((2 * rows + 16, width), BF16),
        in_specs=[pl.BlockSpec(memory_space=VMEM)] * 4,
        out_specs=pl.BlockSpec(memory_space=VMEM),
        compiler_params=params(),
        name="block_weights_and_ids",
    )(p0, p1, my_ids, other_ids)


def pick_kernel(slots, place, hist, out):
    item = place[0]
    owners = out.shape[0]
    users = out.shape[1]
    group = hist.shape[0]

    def one(owner, carry):
        for slot in range(users):
            local = slots[(owner * 8 + item) * users + slot] - item * group
            out[owner, slot] = hist[local]
        return carry

    lax.fori_loop(0, owners, one, 0, unroll=4)


def pick(scorer_user, place, hist, owners, users):
    return pl.pallas_call(
        pick_kernel,
        out_shape=jax.ShapeDtypeStruct((owners, users) + hist.shape[1:], hist.dtype),
        in_specs=[
            pl.BlockSpec(memory_space=SMEM),
            pl.BlockSpec(memory_space=SMEM),
            pl.BlockSpec(memory_space=VMEM),
        ],
        out_specs=pl.BlockSpec(memory_space=VMEM),
        compiler_params=params(),
        name="pick_history",
    )(scorer_user, place, hist)


def fetch_kernel(place, gathered, table, *outs):
    item, x = place[0], place[1]
    rows = table.shape[0]
    step = gathered.shape[0] // 4
    parts = []
    for k in range(4):
        at = pl.multiple_of((x + k) % 4 * step + step - 16, 16)
        parts.append(gathered[pl.ds(at, 16), :].astype(F32)[:2])
    digits = jnp.concatenate(parts, axis=0)
    count = digits.shape[1] // 2
    local = digits[:, :count] * 128.0 + digits[:, count:] - (item * rows).astype(F32)
    mine = (local >= 0.0) & (local < float(rows))
    before = (iota((count, count), 0) < iota((count, count), 1)).astype(BF16)
    rank = dot(mine.astype(F32).astype(BF16), before)
    key = jnp.where(mine, rank, -1.0)
    tab = table[...]
    slot = iota((CAP, count), 0).astype(F32)
    for k in range(8):
        match = slot == key[k : k + 1]
        row_of = jnp.sum(jnp.where(match, local[k : k + 1], 0.0), axis=1, keepdims=True)
        hot = (iota((CAP, rows), 1).astype(F32) == row_of).astype(BF16)
        at = (k % 2) * CAP
        outs[k // 2][at : at + CAP] = dot(hot, tab).astype(BF16)


def fetch(place, gathered, table):
    return pl.pallas_call(
        fetch_kernel,
        out_shape=(jax.ShapeDtypeStruct((2 * CAP, table.shape[1]), table.dtype),) * 4,
        in_specs=[pl.BlockSpec(memory_space=SMEM)] + [pl.BlockSpec(memory_space=VMEM)] * 2,
        out_specs=(pl.BlockSpec(memory_space=VMEM),) * 4,
        compiler_params=params(),
        name="fetch_rows",
    )(place, gathered, table)


def strip_kernel(gathered, out):
    step, keep = gathered.shape[0] // 4, out.shape[0] // 4
    for k in range(4):
        out[k * keep : (k + 1) * keep] = gathered[k * step : k * step + keep]


def strip(gathered):
    rows, width = gathered.shape
    return pl.pallas_call(
        strip_kernel,
        out_shape=jax.ShapeDtypeStruct((rows - 64, width), BF16),
        in_specs=[pl.BlockSpec(memory_space=VMEM)],
        out_specs=pl.BlockSpec(memory_space=VMEM),
        compiler_params=params(),
        name="strip_ids",
    )(gathered)


def pack_kernel(starts, *refs):
    out = refs[-1]
    at = 0
    for start, ref in zip(starts, refs[:-1]):
        rows = ref.shape[0] - start
        out[at : at + rows] = ref[start:]
        at += rows


def pack(starts, pieces):
    rows = sum(piece.shape[0] - start for start, piece in zip(starts, pieces))
    return pl.pallas_call(
        functools.partial(pack_kernel, starts),
        out_shape=jax.ShapeDtypeStruct((rows, pieces[0].shape[1]), BF16),
        in_specs=[pl.BlockSpec(memory_space=VMEM)] * len(pieces),
        out_specs=pl.BlockSpec(memory_space=VMEM),
        compiler_params=params(),
        name="pack_for_core",
    )(*pieces)


def proj_kernel(
    place, cand, w0, w1, w2a, w2b, w3, other, gate, query, self_term, out_weight
):
    core = place[2]
    rows, width = cand.shape
    values = cand[...].astype(F32)
    center = values - jnp.mean(values, axis=-1, keepdims=True)
    spread = jnp.mean(center * center, axis=-1, keepdims=True)
    normed = (center * lax.rsqrt(spread + 1e-06)).astype(BF16)
    g = iota((width, width), 1)
    peer = (g // 16) % 4 * 2 + (core + g // 256) % 2
    from_z = (place[4] + 32 - peer - (g // 8) % 2 * 8) % 16
    from_y = (place[3] + 4 - (g // 64) % 4) % 4
    natural = from_z * 32 + from_y * 8 + g % 8
    perm = (iota((width, width), 0) == natural).astype(BF16)
    normed = dot(normed, perm).astype(BF16)
    shard = w0.shape[0]

    def weight(cols):
        parts = [(k * 5 + cols) * 16 for k in range(4)]
        own = [(ref, at) for ref in (w0, w1) for at in parts]
        own += [(w2a, parts[0]), (w2a, parts[1])]
        own += [(w2b, parts[2] - shard // 2), (w2b, parts[3] - shard // 2)]
        own += [(w3, at) for at in parts]
        own += [(other, k * shard + at) for k in range(4) for at in parts]
        return jnp.concatenate([ref[at : at + 16] for ref, at in own], axis=0)

    out_weight[...] = dot(perm, weight(4)).astype(BF16)
    gate[...] = silu(dot(normed, weight(0)))
    value = silu(dot(normed, weight(1))).astype(BF16).astype(F32)
    q = silu(dot(normed, weight(2))).astype(BF16)
    k = silu(dot(normed, weight(3))).astype(BF16)
    query[...] = q
    product = q.astype(F32) * k.astype(F32)
    head = width // HEADS
    for h in range(HEADS):
        cols = slice(h * head, (h + 1) * head)
        score = jnp.sum(product[:, cols], axis=-1, keepdims=True) * head ** (-0.5)
        self_term[:, cols] = silu(score).astype(BF16).astype(F32) * value[:, cols]


def project(place, cand, pieces, other):
    rows, width = cand.shape
    return pl.pallas_call(
        proj_kernel,
        out_shape=(
            jax.ShapeDtypeStruct((rows, width), F32),
            jax.ShapeDtypeStruct((rows, width), BF16),
            jax.ShapeDtypeStruct((rows, width), F32),
            jax.ShapeDtypeStruct((width, width), BF16),
        ),
        in_specs=[pl.BlockSpec(memory_space=SMEM)] + [pl.BlockSpec(memory_space=VMEM)] * 7,
        out_specs=(pl.BlockSpec(memory_space=VMEM),) * 4,
        compiler_params=params(),
        name="project",
        cost_estimate=pl.CostEstimate(flops=int(2e10), bytes_accessed=0, transcendentals=0),
    )(place, cand, *pieces, other)


def order_kernel(place, ids, f0, f1, f2, f3, other, out):
    own = (f0, f1, f2, f3)
    x, core = place[1], place[2]
    rows, width = out.shape
    shard = ids[...] // 1024
    before = (iota((rows, rows), 0) < iota((rows, rows), 1)).astype(BF16)
    hot = iota((8, rows), 0) == shard
    ranks = dot(hot.astype(BF16), before)
    rank = jnp.sum(jnp.where(hot, ranks, 0.0), axis=0, keepdims=True)
    offset = ((x + 4 - shard // 2) % 4) * 2 + (core + 2 - shard % 2) % 2
    total = jnp.zeros((rows, width), F32)
    for j in range(8):
        key = jnp.where(offset == j, rank, -1.0)
        chosen = (iota((CAP, rows), 0).astype(F32) == key).astype(BF16)
        at = other.shape[0] - (4 - j // 2) * CAP
        piece = other[at : at + CAP] if j % 2 else own[j // 2][:CAP]
        total += lax.dot_general(
            chosen, piece, (((0,), (0,)), ((), ())), preferred_element_type=F32
        )
    out[...] = total.astype(BF16)


def order(place, ids, pieces, other):
    return pl.pallas_call(
        order_kernel,
        out_shape=jax.ShapeDtypeStruct((ids.shape[1], other.shape[1]), BF16),
        in_specs=[pl.BlockSpec(memory_space=SMEM)] + [pl.BlockSpec(memory_space=VMEM)] * 6,
        out_specs=pl.BlockSpec(memory_space=VMEM),
        compiler_params=params(),
        name="order_rows",
    )(place, ids, *pieces, other)


def score_kernel(lengths, hist, query, self_term, gate, cand, out_weight, rows_ref, out):
    owners, users, per_owner, _ = hist.shape
    width = cand.shape[1]
    head = width // HEADS
    positions = owners * per_owner
    count = cand.shape[0] // users
    lane = iota((1, positions), 1)
    position = (lane % per_owner) * owners + lane // per_owner
    for user in range(users):
        at = slice(user * count, (user + 1) * count)
        length = lengths[user]
        live = position < length
        kv = hist[:, user].reshape(positions, 2 * width)
        parts = []
        for h in range(HEADS):
            cols = slice(h * head, (h + 1) * head)
            scores = lax.dot_general(
                query[at, cols], kv[:, cols], (((1,), (1,)), ((), ())), preferred_element_type=F32
            ) * (head ** (-0.5))
            weights = jnp.where(live, silu(scores), 0.0).astype(BF16)
            parts.append(dot(weights, kv[:, width + h * head : width + (h + 1) * head]))
        attended = (jnp.concatenate(parts, axis=1) + self_term[at]) / (
            length.astype(F32) + 1.0
        )
        center = attended - jnp.mean(attended, axis=-1, keepdims=True)
        spread = jnp.mean(center * center, axis=-1, keepdims=True)
        gated = (center * lax.rsqrt(spread + 1e-06) * gate[at]).astype(BF16)
        final = cand[at].astype(F32) + dot(gated, out_weight[...])
        scale = lax.rsqrt(jnp.mean(final * final, axis=-1, keepdims=True) + 1e-06)
        unit = (final * scale).astype(BF16).astype(F32)
        logit = jnp.sum(unit * rows_ref[at].astype(F32), axis=-1, keepdims=True)
        eye = iota((count, count), 0) == iota((count, count), 1)
        out[user : user + 1, :] = jnp.sum(jnp.where(eye, logit, 0.0), axis=0, keepdims=True)


def score(lengths, hist, query, self_term, gate, cand, out_weight, rows):
    users = hist.shape[1]
    return pl.pallas_call(
        score_kernel,
        out_shape=jax.ShapeDtypeStruct((users, cand.shape[0] // users), F32),
        in_specs=[pl.BlockSpec(memory_space=SMEM)] + [pl.BlockSpec(memory_space=VMEM)] * 7,
        out_specs=pl.BlockSpec(memory_space=VMEM),
        compiler_params=params(),
        name="score",
    )(lengths, hist, query, self_term, gate, cand, out_weight, rows)


def along(axis, values, offset):
    size = lax.axis_size(axis)
    return lax.ppermute(values, axis, [(j, (j + offset) % size) for j in range(size)])


def swap_core(values):
    return lax.ppermute(values, "core", [(0, 1), (1, 0)])


def body(
    candidates, proj_weight, out_weight, history_kv, scorer_user, hist_len, cand_item, item_table
):
    users, count, width = candidates.shape
    cand = candidates.reshape(users * count, width)
    x, core = lax.axis_index("x"), lax.axis_index("core")
    item = x * 2 + core
    y, z = lax.axis_index("y"), lax.axis_index("z")
    place = jnp.stack([item, x, core, y, z]).astype(jnp.int32)
    owners = lax.axis_size(USER)

    shard = stack_shard(proj_weight, out_weight)
    zs, items = lax.axis_size("z"), lax.axis_size(ITEM)
    shards = [
        lax.ppermute(
            shard,
            ("z",) + ITEM,
            [
                (k * items + i, (k + i + step) % zs * items + i)
                for k in range(zs)
                for i in range(items)
            ],
        )
        for step in (8, 0)
    ][::-1]
    my_ids = cand_item.reshape(1, users * count)
    other_ids = swap_core(my_ids)

    hist = history_kv.reshape(history_kv.shape[0], history_kv.shape[1], -1)
    picked = pick(scorer_user, place, hist, owners, users)
    arrived = lax.all_to_all(picked, USER, split_axis=0, concat_axis=0, tiled=True)

    gathered = lax.all_gather(block(*shards, my_ids, other_ids), "x", axis=0, tiled=True)
    weight = strip(gathered)
    half = weight.shape[0] // 2
    left, right = along("y", weight, 1), along("y", weight, 3)
    far_top, far_end = along("y", left[:half], 1), along("y", right[half:], 3)
    pieces = [weight, left, far_top, far_end, right]

    found = list(fetch(place, gathered, item_table))
    for k in (1, 3, 2):
        found[k] = along("x", found[k], k)
    other = swap_core(pack((0,) * 5 + (CAP,) * 4, pieces + found))
    gate, query, self_term, out_w = project(place, cand, pieces, other)
    rows = order(place, my_ids, found, other)
    return score(hist_len, arrived, query, self_term, gate, cand, out_w, rows)


def solution(mesh):
    cut = Mesh(mesh.devices.reshape(16, 4, 4, 2), ("z", "y", "x", "core"))
    return jax.shard_map(
        body,
        mesh=cut,
        in_specs=(
            P(USER + ITEM, None, None),
            P(USER, None),
            P(USER, None),
            P(ITEM, None, USER, None),
            P(),
            P(USER + ITEM),
            P(USER + ITEM, None),
            P(ITEM, None),
        ),
        out_specs=P(USER + ITEM, None),
        check_vma=False,
    )
```

```python
import functools

import jax
import jax.numpy as jnp
from jax import lax
from jax.experimental import pallas as pl
from jax.experimental.pallas import tpu as pltpu
from jax.sharding import Mesh, PartitionSpec as P

HEADS = 4
CAP = 96
F32 = jnp.float32
BF16 = jnp.bfloat16
VMEM = pltpu.VMEM
SMEM = pltpu.SMEM
VMEM_LIMIT = 40 * 1024 * 1024
PICK_LIMIT = 60 * 1024 * 1024

USER = ("z", "y")
ITEM = ("x", "core")


def params():
    return pltpu.CompilerParams(vmem_limit_bytes=VMEM_LIMIT)


def silu(values):
    half = 0.5 * values
    return half + half * jnp.tanh(half)


def iota(shape, dim):
    return lax.broadcasted_iota(jnp.int32, shape, dim)


def dot(a, b):
    return jnp.dot(a, b, preferred_element_type=F32)


def block_kernel(p0, p1, my_ids, other_ids, out):
    rows = jnp.concatenate([p0[...].astype(F32), p1[...].astype(F32)], axis=0).astype(BF16)
    count = rows.shape[0]
    k = iota((count, count), 0)
    source = (k % 16) // 8 * (count // 2) + k // 16 * 8 + k % 8
    move = (iota((count, count), 1) == source).astype(BF16)
    ids = jnp.concatenate([my_ids[...], other_ids[...]], axis=0)
    digits = jnp.concatenate([ids // 128, ids % 128], axis=1).astype(F32)
    rest = jnp.zeros((out.shape[0] - count - 2, out.shape[1]), F32)
    out[...] = jnp.concatenate([dot(move, rows), digits, rest], axis=0).astype(BF16)


def block(p0, p1, my_ids, other_ids):
    rows, width = p0.shape
    return pl.pallas_call(
        block_kernel,
        out_shape=jax.ShapeDtypeStruct((2 * rows + 16, width), BF16),
        in_specs=[pl.BlockSpec(memory_space=VMEM)] * 4,
        out_specs=pl.BlockSpec(memory_space=VMEM),
        compiler_params=params(),
        name="block_weights_and_ids",
    )(p0, p1, my_ids, other_ids)


def pick_kernel(slots, place, proj_weight, out_weight, hist, shard, out):
    width = shard.shape[1]
    wide = proj_weight[...].astype(F32)
    parts = [wide[:, k * width : (k + 1) * width] for k in range(4)]
    parts.append(out_weight[...].astype(F32))
    shard[...] = jnp.concatenate(parts, axis=0).astype(BF16)
    item = place[0]
    owners, users = out.shape[0], out.shape[1]
    group = hist.shape[0]

    def one(owner, carry):
        for slot in range(users):
            local = slots[(owner * 8 + item) * users + slot] - item * group
            out[owner, slot] = hist[local]
        return carry

    lax.fori_loop(0, owners, one, 0, unroll=8)


def pick(scorer_user, place, proj_weight, out_weight, hist, owners, users):
    rows, width = out_weight.shape
    return pl.pallas_call(
        pick_kernel,
        out_shape=(
            jax.ShapeDtypeStruct((rows * 5, width), BF16),
            jax.ShapeDtypeStruct((owners, users) + hist.shape[1:], hist.dtype),
        ),
        in_specs=[pl.BlockSpec(memory_space=SMEM)] * 2 + [pl.BlockSpec(memory_space=VMEM)] * 3,
        out_specs=(pl.BlockSpec(memory_space=VMEM),) * 2,
        compiler_params=pltpu.CompilerParams(vmem_limit_bytes=PICK_LIMIT),
        name="stack_and_pick",
    )(scorer_user, place, proj_weight, out_weight, hist)


def later_kernel(first, values, out):
    out[...] = values[...]


def later(first, values):
    return pl.pallas_call(
        later_kernel,
        out_shape=jax.ShapeDtypeStruct(values.shape, values.dtype),
        in_specs=[pl.BlockSpec(memory_space=pl.ANY), pl.BlockSpec(memory_space=VMEM)],
        out_specs=pl.BlockSpec(memory_space=VMEM),
        compiler_params=params(),
        name="ids_later",
    )(first, values)


def fetch_kernel(place, gathered, table, *outs):
    item, x = place[0], place[1]
    rows = table.shape[0]
    step = gathered.shape[0] // 4
    parts = []
    for k in range(4):
        at = pl.multiple_of((x + k) % 4 * step + step - 16, 16)
        parts.append(gathered[pl.ds(at, 16), :].astype(F32)[:2])
    digits = jnp.concatenate(parts, axis=0)
    count = digits.shape[1] // 2
    local = digits[:, :count] * 128.0 + digits[:, count:] - (item * rows).astype(F32)
    mine = (local >= 0.0) & (local < float(rows))
    before = (iota((count, count), 0) < iota((count, count), 1)).astype(BF16)
    rank = dot(mine.astype(F32).astype(BF16), before)
    key = jnp.where(mine, rank, -1.0)
    tab = table[...]
    slot = iota((CAP, count), 0).astype(F32)
    for k in range(8):
        match = slot == key[k : k + 1]
        row_of = jnp.sum(jnp.where(match, local[k : k + 1], 0.0), axis=1, keepdims=True)
        hot = (iota((CAP, rows), 1).astype(F32) == row_of).astype(BF16)
        at = (k % 2) * CAP
        outs[k // 2][at : at + CAP] = dot(hot, tab).astype(BF16)


def fetch(place, gathered, table):
    return pl.pallas_call(
        fetch_kernel,
        out_shape=(jax.ShapeDtypeStruct((2 * CAP, table.shape[1]), table.dtype),) * 4,
        in_specs=[pl.BlockSpec(memory_space=SMEM)] + [pl.BlockSpec(memory_space=VMEM)] * 2,
        out_specs=(pl.BlockSpec(memory_space=VMEM),) * 4,
        compiler_params=params(),
        name="fetch_rows",
    )(place, gathered, table)


def strip_kernel(gathered, out):
    step, keep = gathered.shape[0] // 4, out.shape[0] // 4
    for k in range(4):
        out[k * keep : (k + 1) * keep] = gathered[k * step : k * step + keep]


def strip(gathered):
    rows, width = gathered.shape
    return pl.pallas_call(
        strip_kernel,
        out_shape=jax.ShapeDtypeStruct((rows - 64, width), BF16),
        in_specs=[pl.BlockSpec(memory_space=VMEM)],
        out_specs=pl.BlockSpec(memory_space=VMEM),
        compiler_params=params(),
        name="strip_ids",
    )(gathered)


def pack_kernel(starts, *refs):
    out = refs[-1]
    at = 0
    for start, ref in zip(starts, refs[:-1]):
        rows = ref.shape[0] - start
        out[at : at + rows] = ref[start:]
        at += rows


def pack(starts, pieces):
    rows = sum(piece.shape[0] - start for start, piece in zip(starts, pieces))
    return pl.pallas_call(
        functools.partial(pack_kernel, starts),
        out_shape=jax.ShapeDtypeStruct((rows, pieces[0].shape[1]), BF16),
        in_specs=[pl.BlockSpec(memory_space=VMEM)] * len(pieces),
        out_specs=pl.BlockSpec(memory_space=VMEM),
        compiler_params=params(),
        name="pack_for_core",
    )(*pieces)


def natural_rows(place, half, size):
    g = iota((size, size // 2), 1)
    peer = (g // 16) % 4 * 2 + (place[2] + half) % 2
    from_z = (place[4] + 32 - peer - (g // 8) % 2 * 8) % 16
    from_y = (place[3] + 4 - (g // 64) % 4) % 4
    natural = from_z * 32 + from_y * 8 + g % 8
    return (iota((size, size // 2), 0) == natural).astype(BF16)


def row_keys(place, ids):
    rows = ids.shape[1]
    shard = ids // 1024
    before = (iota((rows, rows), 0) < iota((rows, rows), 1)).astype(BF16)
    hot = iota((8, rows), 0) == shard
    ranks = dot(hot.astype(BF16), before)
    rank = jnp.sum(jnp.where(hot, ranks, 0.0), axis=0, keepdims=True)
    offset = ((place[1] + 4 - shard // 2) % 4) * 2 + (place[2] + 2 - shard % 2) % 2
    return rank, offset


def place_rows(rank, offset, at, piece):
    key = jnp.where(offset == at, rank, -1.0)
    chosen = (iota((CAP, rank.shape[1]), 0).astype(F32) == key).astype(BF16)
    return lax.dot_general(
        chosen, piece, (((0,), (0,)), ((), ())), preferred_element_type=F32
    )


def own_kernel(
    place, ids, cand, w0, w1, w2a, w2b, w3, f0, f1, f2, f3, part, rest, out_weight, rows_out
):
    width = cand.shape[1]
    values = cand[...].astype(F32)
    center = values - jnp.mean(values, axis=-1, keepdims=True)
    spread = jnp.mean(center * center, axis=-1, keepdims=True)
    normed = (center * lax.rsqrt(spread + 1e-06)).astype(BF16)
    rest[...] = dot(normed, natural_rows(place, 1, width)).astype(BF16)
    perm = natural_rows(place, 0, width)
    normed = dot(normed, perm).astype(BF16)
    shard = w0.shape[0]

    def weight(cols):
        parts = [(k * 5 + cols) * 16 for k in range(4)]
        own = [(ref, at) for ref in (w0, w1) for at in parts]
        own += [(w2a, parts[0]), (w2a, parts[1])]
        own += [(w2b, parts[2] - shard // 2), (w2b, parts[3] - shard // 2)]
        own += [(w3, at) for at in parts]
        return jnp.concatenate([ref[at : at + 16] for ref, at in own], axis=0)

    out_weight[...] = dot(perm, weight(4)).astype(BF16)
    for k in range(4):
        part[:, k * width : (k + 1) * width] = dot(normed, weight(k))
    rank, offset = row_keys(place, ids[...])
    total = place_rows(rank, offset, 0, f0[:CAP]) + place_rows(rank, offset, 2, f1[:CAP])
    total += place_rows(rank, offset, 4, f2[:CAP]) + place_rows(rank, offset, 6, f3[:CAP])
    rows_out[...] = total.astype(BF16)


def project_own(place, ids, cand, pieces, found):
    rows, width = cand.shape
    return pl.pallas_call(
        own_kernel,
        out_shape=(
            jax.ShapeDtypeStruct((rows, 4 * width), F32),
            jax.ShapeDtypeStruct((rows, width // 2), BF16),
            jax.ShapeDtypeStruct((width, width), BF16),
            jax.ShapeDtypeStruct((rows, width), BF16),
        ),
        in_specs=[pl.BlockSpec(memory_space=SMEM)] + [pl.BlockSpec(memory_space=VMEM)] * 11,
        out_specs=(pl.BlockSpec(memory_space=VMEM),) * 4,
        compiler_params=params(),
        name="project_own",
    )(place, ids, cand, *pieces, *found)


def rest_kernel(
    place, ids, part, rest, own_weight, own_rows, other, gate, query, self_term, out_weight, rows_out
):
    width = own_rows.shape[1]
    shard = (other.shape[0] - 4 * CAP) // 4
    normed = rest[...]

    def weight(cols):
        parts = [k * shard + (x * 5 + cols) * 16 for k in range(4) for x in range(4)]
        return jnp.concatenate([other[at : at + 16] for at in parts], axis=0)

    def proj(k):
        return silu(part[:, k * width : (k + 1) * width] + dot(normed, weight(k)))

    perm = natural_rows(place, 1, width)
    out_weight[...] = own_weight[...] + dot(perm, weight(4)).astype(BF16)
    gate[...] = proj(0)
    value = proj(1).astype(BF16).astype(F32)
    q = proj(2).astype(BF16)
    k = proj(3).astype(BF16)
    query[...] = q
    product = q.astype(F32) * k.astype(F32)
    head = width // HEADS
    for h in range(HEADS):
        cols = slice(h * head, (h + 1) * head)
        score = jnp.sum(product[:, cols], axis=-1, keepdims=True) * head ** (-0.5)
        self_term[:, cols] = silu(score).astype(BF16).astype(F32) * value[:, cols]
    rank, offset = row_keys(place, ids[...])
    total = own_rows[...].astype(F32)
    for k in range(4):
        at = other.shape[0] - (4 - k) * CAP
        total += place_rows(rank, offset, 2 * k + 1, other[at : at + CAP])
    rows_out[...] = total.astype(BF16)


def project_rest(place, ids, own, other):
    rows, width = own[3].shape
    return pl.pallas_call(
        rest_kernel,
        out_shape=(
            jax.ShapeDtypeStruct((rows, width), F32),
            jax.ShapeDtypeStruct((rows, width), BF16),
            jax.ShapeDtypeStruct((rows, width), F32),
            jax.ShapeDtypeStruct((width, width), BF16),
            jax.ShapeDtypeStruct((rows, width), BF16),
        ),
        in_specs=[pl.BlockSpec(memory_space=SMEM)] + [pl.BlockSpec(memory_space=VMEM)] * 6,
        out_specs=(pl.BlockSpec(memory_space=VMEM),) * 5,
        compiler_params=params(),
        name="project",
        cost_estimate=pl.CostEstimate(flops=int(1.9e10), bytes_accessed=0, transcendentals=0),
    )(place, ids, *own, other)


def score_kernel(lengths, hist, query, self_term, gate, cand, out_weight, rows_ref, out):
    owners, users, per_owner, _ = hist.shape
    width = cand.shape[1]
    head = width // HEADS
    positions = owners * per_owner
    count = cand.shape[0] // users
    lane = iota((1, positions), 1)
    position = (lane % per_owner) * owners + lane // per_owner
    for user in range(users):
        at = slice(user * count, (user + 1) * count)
        length = lengths[user]
        live = position < length
        kv = hist[:, user].reshape(positions, 2 * width)
        parts = []
        for h in range(HEADS):
            cols = slice(h * head, (h + 1) * head)
            scores = lax.dot_general(
                query[at, cols], kv[:, cols], (((1,), (1,)), ((), ())), preferred_element_type=F32
            ) * (head ** (-0.5))
            weights = jnp.where(live, silu(scores), 0.0).astype(BF16)
            parts.append(dot(weights, kv[:, width + h * head : width + (h + 1) * head]))
        attended = (jnp.concatenate(parts, axis=1) + self_term[at]) * (
            1.0 / (length.astype(F32) + 1.0)
        )
        center = attended - jnp.mean(attended, axis=-1, keepdims=True)
        spread = jnp.mean(center * center, axis=-1, keepdims=True)
        gated = (center * lax.rsqrt(spread + 1e-06) * gate[at]).astype(BF16)
        final = cand[at].astype(F32) + dot(gated, out_weight[...])
        scale = lax.rsqrt(jnp.mean(final * final, axis=-1, keepdims=True) + 1e-06)
        unit = (final * scale).astype(BF16).astype(F32)
        logit = jnp.sum(unit * rows_ref[at].astype(F32), axis=-1, keepdims=True)
        eye = iota((count, count), 0) == iota((count, count), 1)
        out[user : user + 1, :] = jnp.sum(jnp.where(eye, logit, 0.0), axis=0, keepdims=True)


def score(lengths, hist, query, self_term, gate, cand, out_weight, rows):
    users = hist.shape[1]
    return pl.pallas_call(
        score_kernel,
        out_shape=jax.ShapeDtypeStruct((users, cand.shape[0] // users), F32),
        in_specs=[pl.BlockSpec(memory_space=SMEM)] + [pl.BlockSpec(memory_space=VMEM)] * 7,
        out_specs=pl.BlockSpec(memory_space=VMEM),
        compiler_params=params(),
        name="score",
    )(lengths, hist, query, self_term, gate, cand, out_weight, rows)


def along(axis, values, offset):
    size = lax.axis_size(axis)
    return lax.ppermute(values, axis, [(j, (j + offset) % size) for j in range(size)])


def swap_core(values):
    return lax.ppermute(values, "core", [(0, 1), (1, 0)])


def body(
    candidates, proj_weight, out_weight, history_kv, scorer_user, hist_len, cand_item, item_table
):
    users, count, width = candidates.shape
    cand = candidates.reshape(users * count, width)
    x, core = lax.axis_index("x"), lax.axis_index("core")
    item = x * 2 + core
    y, z = lax.axis_index("y"), lax.axis_index("z")
    place = jnp.stack([item, x, core, y, z]).astype(jnp.int32)
    owners = lax.axis_size(USER)

    hist = history_kv.reshape(history_kv.shape[0], history_kv.shape[1], -1)
    shard, picked = pick(scorer_user, place, proj_weight, out_weight, hist, owners, users)

    zs, items = lax.axis_size("z"), lax.axis_size(ITEM)
    shards = [
        lax.ppermute(
            shard,
            ("z",) + ITEM,
            [
                (k * items + i, (k + i + step) % zs * items + i)
                for k in range(zs)
                for i in range(items)
            ],
        )
        for step in (8, 0)
    ][::-1]

    arrived = lax.all_to_all(picked, USER, split_axis=0, concat_axis=0, tiled=True)

    my_ids = cand_item.reshape(1, users * count)
    other_ids = swap_core(later(picked, my_ids))

    gathered = lax.all_gather(block(*shards, my_ids, other_ids), "x", axis=0, tiled=True)
    weight = strip(gathered)
    half = weight.shape[0] // 2
    left, right = along("y", weight, 1), along("y", weight, 3)
    far_top, far_end = along("y", left[:half], 1), along("y", right[half:], 3)
    pieces = [weight, left, far_top, far_end, right]

    found = list(fetch(place, gathered, item_table))
    for k in (1, 3, 2):
        found[k] = along("x", found[k], k)
    other = swap_core(pack((0,) * 5 + (CAP,) * 4, pieces + found))
    own = project_own(place, my_ids, cand, pieces, found)
    gate, query, self_term, out_w, rows = project_rest(place, my_ids, own, other)
    return score(hist_len, arrived, query, self_term, gate, cand, out_w, rows)


def solution(mesh):
    cut = Mesh(mesh.devices.reshape(16, 4, 4, 2), ("z", "y", "x", "core"))
    return jax.shard_map(
        body,
        mesh=cut,
        in_specs=(
            P(USER + ITEM, None, None),
            P(USER, None),
            P(USER, None),
            P(ITEM, None, USER, None),
            P(),
            P(USER + ITEM),
            P(USER + ITEM, None),
            P(ITEM, None),
        ),
        out_specs=P(USER + ITEM, None),
        check_vma=False,
    )
```

```python
import functools

import jax
import jax.numpy as jnp
from jax import lax
from jax.experimental import pallas as pl
from jax.experimental.pallas import tpu as pltpu
from jax.sharding import Mesh, PartitionSpec as P

HEADS = 4
CAP = 96
F32 = jnp.float32
BF16 = jnp.bfloat16
VMEM = pltpu.VMEM
SMEM = pltpu.SMEM
VMEM_LIMIT = 40 * 1024 * 1024
PICK_LIMIT = 60 * 1024 * 1024

USER = ("z", "y")
ITEM = ("x", "core")


def params():
    return pltpu.CompilerParams(vmem_limit_bytes=VMEM_LIMIT)


def silu(values):
    half = 0.5 * values
    return half + half * jnp.tanh(half)


def iota(shape, dim):
    return lax.broadcasted_iota(jnp.int32, shape, dim)


def dot(a, b):
    return jnp.dot(a, b, preferred_element_type=F32)


def block_kernel(p0, p1, my_ids, other_ids, out):
    rows = jnp.concatenate([p0[...].astype(F32), p1[...].astype(F32)], axis=0).astype(BF16)
    count = rows.shape[0]
    k = iota((count, count), 0)
    source = (k % 16) // 8 * (count // 2) + k // 16 * 8 + k % 8
    move = (iota((count, count), 1) == source).astype(BF16)
    ids = jnp.concatenate([my_ids[...], other_ids[...]], axis=0)
    digits = jnp.concatenate([ids // 128, ids % 128], axis=1).astype(F32)
    rest = jnp.zeros((out.shape[0] - count - 2, out.shape[1]), F32)
    out[...] = jnp.concatenate([dot(move, rows), digits, rest], axis=0).astype(BF16)


def block(p0, p1, my_ids, other_ids):
    rows, width = p0.shape
    return pl.pallas_call(
        block_kernel,
        out_shape=jax.ShapeDtypeStruct((2 * rows + 16, width), BF16),
        in_specs=[pl.BlockSpec(memory_space=VMEM)] * 4,
        out_specs=pl.BlockSpec(memory_space=VMEM),
        compiler_params=params(),
        name="block_weights_and_ids",
    )(p0, p1, my_ids, other_ids)


def pick_kernel(slots, place, proj_weight, out_weight, hist, shard, out):
    width = shard.shape[1]
    wide = proj_weight[...].astype(F32)
    parts = [wide[:, k * width : (k + 1) * width] for k in range(4)]
    parts.append(out_weight[...].astype(F32))
    shard[...] = jnp.concatenate(parts, axis=0).astype(BF16)
    item = place[0]
    owners, users = out.shape[0], out.shape[1]
    group = hist.shape[0]

    def one(owner, carry):
        for slot in range(users):
            local = slots[(owner * 8 + item) * users + slot] - item * group
            out[owner, slot] = hist[local]
        return carry

    lax.fori_loop(0, owners, one, 0, unroll=8)


def pick(scorer_user, place, proj_weight, out_weight, hist, owners, users):
    rows, width = out_weight.shape
    return pl.pallas_call(
        pick_kernel,
        out_shape=(
            jax.ShapeDtypeStruct((rows * 5, width), BF16),
            jax.ShapeDtypeStruct((owners, users) + hist.shape[1:], hist.dtype),
        ),
        in_specs=[pl.BlockSpec(memory_space=SMEM)] * 2 + [pl.BlockSpec(memory_space=VMEM)] * 3,
        out_specs=(pl.BlockSpec(memory_space=VMEM),) * 2,
        compiler_params=pltpu.CompilerParams(vmem_limit_bytes=PICK_LIMIT),
        name="stack_and_pick",
    )(scorer_user, place, proj_weight, out_weight, hist)


def later_kernel(first, values, out):
    out[...] = values[...]


def later(first, values):
    return pl.pallas_call(
        later_kernel,
        out_shape=jax.ShapeDtypeStruct(values.shape, values.dtype),
        in_specs=[pl.BlockSpec(memory_space=pl.ANY), pl.BlockSpec(memory_space=VMEM)],
        out_specs=pl.BlockSpec(memory_space=VMEM),
        compiler_params=params(),
        name="ids_later",
    )(first, values)


def fetch_kernel(place, gathered, table, *outs):
    item, x = place[0], place[1]
    rows = table.shape[0]
    step = gathered.shape[0] // 4
    parts = []
    for k in range(4):
        at = pl.multiple_of((x + k) % 4 * step + step - 16, 16)
        parts.append(gathered[pl.ds(at, 16), :].astype(F32)[:2])
    digits = jnp.concatenate(parts, axis=0)
    count = digits.shape[1] // 2
    local = digits[:, :count] * 128.0 + digits[:, count:] - (item * rows).astype(F32)
    mine = (local >= 0.0) & (local < float(rows))
    before = (iota((count, count), 0) < iota((count, count), 1)).astype(BF16)
    rank = dot(mine.astype(F32).astype(BF16), before)
    key = jnp.where(mine, rank, -1.0)
    slot = iota((CAP, count), 0).astype(F32)
    column = iota((CAP, rows), 1).astype(F32)
    hot = []
    for k in range(8):
        match = slot == key[k : k + 1]
        row_of = jnp.sum(jnp.where(match, local[k : k + 1], 0.0), axis=1, keepdims=True)
        hot.append((column == row_of).astype(BF16))
    found = dot(jnp.concatenate(hot, axis=0), table[...]).astype(BF16)
    for k, out in enumerate(outs):
        out[...] = found[2 * k * CAP : 2 * (k + 1) * CAP]


def fetch(place, gathered, table):
    return pl.pallas_call(
        fetch_kernel,
        out_shape=(jax.ShapeDtypeStruct((2 * CAP, table.shape[1]), table.dtype),) * 4,
        in_specs=[pl.BlockSpec(memory_space=SMEM)] + [pl.BlockSpec(memory_space=VMEM)] * 2,
        out_specs=(pl.BlockSpec(memory_space=VMEM),) * 4,
        compiler_params=params(),
        name="fetch_rows",
    )(place, gathered, table)


def strip_kernel(gathered, out):
    step, keep = gathered.shape[0] // 4, out.shape[0] // 4
    for k in range(4):
        out[k * keep : (k + 1) * keep] = gathered[k * step : k * step + keep]


def strip(gathered):
    rows, width = gathered.shape
    return pl.pallas_call(
        strip_kernel,
        out_shape=jax.ShapeDtypeStruct((rows - 64, width), BF16),
        in_specs=[pl.BlockSpec(memory_space=VMEM)],
        out_specs=pl.BlockSpec(memory_space=VMEM),
        compiler_params=params(),
        name="strip_ids",
    )(gathered)


def pack_kernel(starts, *refs):
    out = refs[-1]
    at = 0
    for start, ref in zip(starts, refs[:-1]):
        rows = ref.shape[0] - start
        out[at : at + rows] = ref[start:]
        at += rows


def pack(starts, pieces):
    rows = sum(piece.shape[0] - start for start, piece in zip(starts, pieces))
    return pl.pallas_call(
        functools.partial(pack_kernel, starts),
        out_shape=jax.ShapeDtypeStruct((rows, pieces[0].shape[1]), BF16),
        in_specs=[pl.BlockSpec(memory_space=VMEM)] * len(pieces),
        out_specs=pl.BlockSpec(memory_space=VMEM),
        compiler_params=params(),
        name="pack_for_core",
    )(*pieces)


def natural_rows(place, half, size):
    g = iota((size, size // 2), 1)
    peer = (g // 16) % 4 * 2 + (place[2] + half) % 2
    from_z = (place[4] + 32 - peer - (g // 8) % 2 * 8) % 16
    from_y = (place[3] + 4 - (g // 64) % 4) % 4
    natural = from_z * 32 + from_y * 8 + g % 8
    return (iota((size, size // 2), 0) == natural).astype(BF16)


def row_keys(place, ids):
    rows = ids.shape[1]
    shard = ids // 1024
    before = (iota((rows, rows), 0) < iota((rows, rows), 1)).astype(BF16)
    hot = iota((8, rows), 0) == shard
    ranks = dot(hot.astype(BF16), before)
    rank = jnp.sum(jnp.where(hot, ranks, 0.0), axis=0, keepdims=True)
    offset = ((place[1] + 4 - shard // 2) % 4) * 2 + (place[2] + 2 - shard % 2) % 2
    return rank, offset


def place_rows(rank, offset, first, pieces):
    slot = iota((CAP, rank.shape[1]), 0).astype(F32)
    chosen = [
        (slot == jnp.where(offset == first + 2 * k, rank, -1.0)).astype(BF16)
        for k in range(len(pieces))
    ]
    return lax.dot_general(
        jnp.concatenate(chosen, axis=0),
        jnp.concatenate(pieces, axis=0),
        (((0,), (0,)), ((), ())),
        preferred_element_type=F32,
    )


def own_kernel(
    place, ids, cand, w0, w1, w2a, w2b, w3, f0, f1, f2, f3, part, rest, out_weight, rows_out
):
    width = cand.shape[1]
    values = cand[...].astype(F32)
    center = values - jnp.mean(values, axis=-1, keepdims=True)
    spread = jnp.mean(center * center, axis=-1, keepdims=True)
    normed = (center * lax.rsqrt(spread + 1e-06)).astype(BF16)
    rest[...] = dot(normed, natural_rows(place, 1, width)).astype(BF16)
    perm = natural_rows(place, 0, width)
    normed = dot(normed, perm).astype(BF16)
    shard = w0.shape[0]

    def weight(cols):
        parts = [(k * 5 + cols) * 16 for k in range(4)]
        own = [(ref, at) for ref in (w0, w1) for at in parts]
        own += [(w2a, parts[0]), (w2a, parts[1])]
        own += [(w2b, parts[2] - shard // 2), (w2b, parts[3] - shard // 2)]
        own += [(w3, at) for at in parts]
        return jnp.concatenate([ref[at : at + 16] for ref, at in own], axis=0)

    out_weight[...] = dot(perm, weight(4)).astype(BF16)
    for k in range(4):
        part[:, k * width : (k + 1) * width] = dot(normed, weight(k))
    rank, offset = row_keys(place, ids[...])
    total = place_rows(rank, offset, 0, [f0[:CAP], f1[:CAP], f2[:CAP], f3[:CAP]])
    rows_out[...] = total.astype(BF16)


def project_own(place, ids, cand, pieces, found):
    rows, width = cand.shape
    return pl.pallas_call(
        own_kernel,
        out_shape=(
            jax.ShapeDtypeStruct((rows, 4 * width), F32),
            jax.ShapeDtypeStruct((rows, width // 2), BF16),
            jax.ShapeDtypeStruct((width, width), BF16),
            jax.ShapeDtypeStruct((rows, width), BF16),
        ),
        in_specs=[pl.BlockSpec(memory_space=SMEM)] + [pl.BlockSpec(memory_space=VMEM)] * 11,
        out_specs=(pl.BlockSpec(memory_space=VMEM),) * 4,
        compiler_params=params(),
        name="project_own",
    )(place, ids, cand, *pieces, *found)


def rest_kernel(
    place, ids, part, rest, own_weight, own_rows, other, gate, query, self_term, out_weight, rows_out
):
    width = own_rows.shape[1]
    shard = (other.shape[0] - 4 * CAP) // 4
    normed = rest[...]

    def weight(cols):
        parts = [k * shard + (x * 5 + cols) * 16 for k in range(4) for x in range(4)]
        return jnp.concatenate([other[at : at + 16] for at in parts], axis=0)

    def proj(k):
        return silu(part[:, k * width : (k + 1) * width] + dot(normed, weight(k)))

    perm = natural_rows(place, 1, width)
    out_weight[...] = own_weight[...] + dot(perm, weight(4)).astype(BF16)
    gate[...] = proj(0)
    value = proj(1).astype(BF16).astype(F32)
    q = proj(2).astype(BF16)
    k = proj(3).astype(BF16)
    query[...] = q
    product = q.astype(F32) * k.astype(F32)
    head = width // HEADS
    for h in range(HEADS):
        cols = slice(h * head, (h + 1) * head)
        score = jnp.sum(product[:, cols], axis=-1, keepdims=True) * head ** (-0.5)
        self_term[:, cols] = silu(score).astype(BF16).astype(F32) * value[:, cols]
    rank, offset = row_keys(place, ids[...])
    ends = [other.shape[0] - (4 - k) * CAP for k in range(4)]
    theirs = place_rows(rank, offset, 1, [other[at : at + CAP] for at in ends])
    total = own_rows[...].astype(F32) + theirs
    rows_out[...] = total.astype(BF16)


def project_rest(place, ids, own, other):
    rows, width = own[3].shape
    return pl.pallas_call(
        rest_kernel,
        out_shape=(
            jax.ShapeDtypeStruct((rows, width), F32),
            jax.ShapeDtypeStruct((rows, width), BF16),
            jax.ShapeDtypeStruct((rows, width), F32),
            jax.ShapeDtypeStruct((width, width), BF16),
            jax.ShapeDtypeStruct((rows, width), BF16),
        ),
        in_specs=[pl.BlockSpec(memory_space=SMEM)] + [pl.BlockSpec(memory_space=VMEM)] * 6,
        out_specs=(pl.BlockSpec(memory_space=VMEM),) * 5,
        compiler_params=params(),
        name="project",
        cost_estimate=pl.CostEstimate(flops=int(1.9e10), bytes_accessed=0, transcendentals=0),
    )(place, ids, *own, other)


def score_kernel(lengths, hist, query, self_term, gate, cand, out_weight, rows_ref, out):
    owners, users, per_owner, _ = hist.shape
    width = cand.shape[1]
    head = width // HEADS
    positions = owners * per_owner
    count = cand.shape[0] // users
    lane = iota((1, positions), 1)
    position = (lane % per_owner) * owners + lane // per_owner
    both = []
    for user in range(users):
        at = slice(user * count, (user + 1) * count)
        length = lengths[user]
        live = position < length
        kv = hist[:, user].reshape(positions, 2 * width)
        parts = []
        for h in range(HEADS):
            cols = slice(h * head, (h + 1) * head)
            scores = lax.dot_general(
                query[at, cols], kv[:, cols], (((1,), (1,)), ((), ())), preferred_element_type=F32
            ) * (head ** (-0.5))
            weights = jnp.where(live, silu(scores), 0.0).astype(BF16)
            parts.append(dot(weights, kv[:, width + h * head : width + (h + 1) * head]))
        attended = jnp.concatenate(parts, axis=1) + self_term[at]
        both.append(attended * (1.0 / (length.astype(F32) + 1.0)))
    attended = jnp.concatenate(both, axis=0)
    center = attended - jnp.mean(attended, axis=-1, keepdims=True)
    spread = jnp.mean(center * center, axis=-1, keepdims=True)
    gated = (center * gate[...] * lax.rsqrt(spread + 1e-06)).astype(BF16)
    final = cand[...].astype(F32) + dot(gated, out_weight[...])
    match = jnp.sum(final * rows_ref[...].astype(F32), axis=-1, keepdims=True)
    logit = match * lax.rsqrt(jnp.mean(final * final, axis=-1, keepdims=True) + 1e-06)
    eye = iota((count, count), 0) == iota((count, count), 1)
    for user in range(users):
        column = logit[user * count : (user + 1) * count]
        out[user : user + 1, :] = jnp.sum(jnp.where(eye, column, 0.0), axis=0, keepdims=True)


def score(lengths, hist, query, self_term, gate, cand, out_weight, rows):
    users = hist.shape[1]
    return pl.pallas_call(
        score_kernel,
        out_shape=jax.ShapeDtypeStruct((users, cand.shape[0] // users), F32),
        in_specs=[pl.BlockSpec(memory_space=SMEM)] + [pl.BlockSpec(memory_space=VMEM)] * 7,
        out_specs=pl.BlockSpec(memory_space=VMEM),
        compiler_params=params(),
        name="score",
    )(lengths, hist, query, self_term, gate, cand, out_weight, rows)


def along(axis, values, offset):
    size = lax.axis_size(axis)
    return lax.ppermute(values, axis, [(j, (j + offset) % size) for j in range(size)])


def swap_core(values):
    return lax.ppermute(values, "core", [(0, 1), (1, 0)])


def body(
    candidates, proj_weight, out_weight, history_kv, scorer_user, hist_len, cand_item, item_table
):
    users, count, width = candidates.shape
    cand = candidates.reshape(users * count, width)
    x, core = lax.axis_index("x"), lax.axis_index("core")
    item = x * 2 + core
    y, z = lax.axis_index("y"), lax.axis_index("z")
    place = jnp.stack([item, x, core, y, z]).astype(jnp.int32)
    owners = lax.axis_size(USER)

    hist = history_kv.reshape(history_kv.shape[0], history_kv.shape[1], -1)
    shard, picked = pick(scorer_user, place, proj_weight, out_weight, hist, owners, users)

    zs, items = lax.axis_size("z"), lax.axis_size(ITEM)
    shards = [
        lax.ppermute(
            shard,
            ("z",) + ITEM,
            [
                (k * items + i, (k + i + step) % zs * items + i)
                for k in range(zs)
                for i in range(items)
            ],
        )
        for step in (8, 0)
    ][::-1]

    arrived = lax.all_to_all(picked, USER, split_axis=0, concat_axis=0, tiled=True)

    my_ids = cand_item.reshape(1, users * count)
    other_ids = swap_core(later(picked, my_ids))

    gathered = lax.all_gather(block(*shards, my_ids, other_ids), "x", axis=0, tiled=True)
    weight = strip(gathered)
    half = weight.shape[0] // 2
    left, right = along("y", weight, 1), along("y", weight, 3)
    far_top, far_end = along("y", left[:half], 1), along("y", right[half:], 3)
    pieces = [weight, left, far_top, far_end, right]

    found = list(fetch(place, gathered, item_table))
    for k in (1, 3, 2):
        found[k] = along("x", found[k], k)
    other = swap_core(pack((0,) * 5 + (CAP,) * 4, pieces + found))
    own = project_own(place, my_ids, cand, pieces, found)
    gate, query, self_term, out_w, rows = project_rest(place, my_ids, own, other)
    return score(hist_len, arrived, query, self_term, gate, cand, out_w, rows)


def solution(mesh):
    cut = Mesh(mesh.devices.reshape(16, 4, 4, 2), ("z", "y", "x", "core"))
    return jax.shard_map(
        body,
        mesh=cut,
        in_specs=(
            P(USER + ITEM, None, None),
            P(USER, None),
            P(USER, None),
            P(ITEM, None, USER, None),
            P(),
            P(USER + ITEM),
            P(USER + ITEM, None),
            P(ITEM, None),
        ),
        out_specs=P(USER + ITEM, None),
        check_vma=False,
    )
```

```python
import functools

import jax
import jax.numpy as jnp
from jax import lax
from jax.experimental import pallas as pl
from jax.experimental.pallas import tpu as pltpu
from jax.sharding import Mesh, PartitionSpec as P

HEADS = 4
CAP = 96
F32 = jnp.float32
BF16 = jnp.bfloat16
VMEM = pltpu.VMEM
SMEM = pltpu.SMEM
VMEM_LIMIT = 40 * 1024 * 1024
PICK_LIMIT = 60 * 1024 * 1024

USER = ("z", "y")
ITEM = ("x", "core")


def params():
    return pltpu.CompilerParams(vmem_limit_bytes=VMEM_LIMIT)


def silu(values):
    half = 0.5 * values
    return half + half * jnp.tanh(half)


def iota(shape, dim):
    return lax.broadcasted_iota(jnp.int32, shape, dim)


def dot(a, b):
    return jnp.dot(a, b, preferred_element_type=F32)


def block_kernel(p0, p1, ids, out):
    rows = jnp.concatenate([p0[...].astype(F32), p1[...].astype(F32)], axis=0).astype(BF16)
    count = rows.shape[0]
    k = iota((count, count), 0)
    source = (k % 16) // 8 * (count // 2) + k // 16 * 8 + k % 8
    move = (iota((count, count), 1) == source).astype(BF16)
    digits = jnp.concatenate([ids[...] // 128, ids[...] % 128], axis=1).astype(F32)
    rest = jnp.zeros((out.shape[0] - count - 1, out.shape[1]), F32)
    out[...] = jnp.concatenate([dot(move, rows), digits, rest], axis=0).astype(BF16)


def block(p0, p1, ids):
    rows, width = p0.shape
    return pl.pallas_call(
        block_kernel,
        out_shape=jax.ShapeDtypeStruct((2 * rows + 16, width), BF16),
        in_specs=[pl.BlockSpec(memory_space=VMEM)] * 3,
        out_specs=pl.BlockSpec(memory_space=VMEM),
        compiler_params=params(),
        name="block_weights_and_ids",
    )(p0, p1, ids)


def pick_kernel(slots, place, proj_weight, out_weight, hist, shard, out):
    width = shard.shape[1]
    wide = proj_weight[...].astype(F32)
    parts = [wide[:, k * width : (k + 1) * width] for k in range(4)]
    parts.append(out_weight[...].astype(F32))
    shard[...] = jnp.concatenate(parts, axis=0).astype(BF16)
    item = place[0]
    owners, users = out.shape[0], out.shape[1]
    group = hist.shape[0]

    def one(owner, carry):
        for slot in range(users):
            local = slots[(owner * 8 + item) * users + slot] - item * group
            out[owner, slot] = hist[local]
        return carry

    lax.fori_loop(0, owners, one, 0, unroll=8)


def pick(scorer_user, place, proj_weight, out_weight, hist, owners, users):
    rows, width = out_weight.shape
    return pl.pallas_call(
        pick_kernel,
        out_shape=(
            jax.ShapeDtypeStruct((rows * 5, width), BF16),
            jax.ShapeDtypeStruct((owners, users) + hist.shape[1:], hist.dtype),
        ),
        in_specs=[pl.BlockSpec(memory_space=SMEM)] * 2 + [pl.BlockSpec(memory_space=VMEM)] * 3,
        out_specs=(pl.BlockSpec(memory_space=VMEM),) * 2,
        compiler_params=pltpu.CompilerParams(vmem_limit_bytes=PICK_LIMIT),
        name="stack_and_pick",
    )(scorer_user, place, proj_weight, out_weight, hist)


def later_kernel(first, values, out):
    out[...] = values[...]


def later(first, values):
    return pl.pallas_call(
        later_kernel,
        out_shape=jax.ShapeDtypeStruct(values.shape, values.dtype),
        in_specs=[pl.BlockSpec(memory_space=pl.ANY), pl.BlockSpec(memory_space=VMEM)],
        out_specs=pl.BlockSpec(memory_space=VMEM),
        compiler_params=params(),
        name="table_later",
    )(first, values)


def fetch_kernel(place, gathered, table, other_table, *outs):
    x, core = place[1], place[2]
    rows = table.shape[0]
    step = gathered.shape[0] // 4
    parts = []
    for k in range(4):
        at = pl.multiple_of((x + k) % 4 * step + step - 16, 16)
        parts.append(gathered[pl.ds(at, 16), :].astype(F32)[:1])
    digits = jnp.concatenate(parts, axis=0)
    count = digits.shape[1] // 2
    ids = digits[:, :count] * 128.0 + digits[:, count:]
    before = (iota((count, count), 0) < iota((count, count), 1)).astype(BF16)
    slot = iota((CAP, count), 0).astype(F32)
    column = iota((CAP, rows), 1).astype(F32)
    for side, tab in enumerate((table, other_table)):
        local = ids - ((x * 2 + (core + side) % 2) * rows).astype(F32)
        mine = (local >= 0.0) & (local < float(rows))
        rank = dot(mine.astype(F32).astype(BF16), before)
        key = jnp.where(mine, rank, -1.0)
        hot = []
        for k in range(4):
            match = slot == key[k : k + 1]
            row_of = jnp.sum(jnp.where(match, local[k : k + 1], 0.0), axis=1, keepdims=True)
            hot.append((column == row_of).astype(BF16))
        found = dot(jnp.concatenate(hot, axis=0), tab[...]).astype(BF16)
        for k, out in enumerate(outs):
            out[side * CAP : (side + 1) * CAP] = found[k * CAP : (k + 1) * CAP]


def fetch(place, gathered, table, other_table):
    return pl.pallas_call(
        fetch_kernel,
        out_shape=(jax.ShapeDtypeStruct((2 * CAP, table.shape[1]), table.dtype),) * 4,
        in_specs=[pl.BlockSpec(memory_space=SMEM)] + [pl.BlockSpec(memory_space=VMEM)] * 3,
        out_specs=(pl.BlockSpec(memory_space=VMEM),) * 4,
        compiler_params=params(),
        name="fetch_rows",
    )(place, gathered, table, other_table)


def strip_kernel(gathered, first, out):
    step, keep = gathered.shape[0] // 4, out.shape[0] // 4
    for k in range(4):
        out[k * keep : (k + 1) * keep] = gathered[k * step : k * step + keep]


def strip(gathered, first):
    rows, width = gathered.shape
    return pl.pallas_call(
        strip_kernel,
        out_shape=jax.ShapeDtypeStruct((rows - 64, width), BF16),
        in_specs=[pl.BlockSpec(memory_space=VMEM), pl.BlockSpec(memory_space=pl.ANY)],
        out_specs=pl.BlockSpec(memory_space=VMEM),
        compiler_params=params(),
        name="strip_ids",
    )(gathered, first)


def pack_kernel(starts, *refs):
    out = refs[-1]
    at = 0
    for start, ref in zip(starts, refs):
        rows = ref.shape[0] - start
        out[at : at + rows] = ref[start:]
        at += rows


def pack(starts, pieces, first):
    rows = sum(piece.shape[0] - start for start, piece in zip(starts, pieces))
    return pl.pallas_call(
        functools.partial(pack_kernel, starts),
        out_shape=jax.ShapeDtypeStruct((rows, pieces[0].shape[1]), BF16),
        in_specs=[pl.BlockSpec(memory_space=VMEM)] * len(pieces)
        + [pl.BlockSpec(memory_space=pl.ANY)] * len(first),
        out_specs=pl.BlockSpec(memory_space=VMEM),
        compiler_params=params(),
        name="pack_for_core",
    )(*pieces, *first)


def natural_rows(place, half, size):
    g = iota((size, size // 2), 1)
    peer = (g // 16) % 4 * 2 + (place[2] + half) % 2
    from_z = (place[4] + 32 - peer - (g // 8) % 2 * 8) % 16
    from_y = (place[3] + 4 - (g // 64) % 4) % 4
    natural = from_z * 32 + from_y * 8 + g % 8
    return (iota((size, size // 2), 0) == natural).astype(BF16)


def row_keys(place, ids):
    rows = ids.shape[1]
    shard = ids // 1024
    before = (iota((rows, rows), 0) < iota((rows, rows), 1)).astype(BF16)
    hot = iota((8, rows), 0) == shard
    ranks = dot(hot.astype(BF16), before)
    rank = jnp.sum(jnp.where(hot, ranks, 0.0), axis=0, keepdims=True)
    offset = ((place[1] + 4 - shard // 2) % 4) * 2 + (place[2] + 2 - shard % 2) % 2
    return rank, offset


def place_rows(rank, offset, first, pieces):
    slot = iota((CAP, rank.shape[1]), 0).astype(F32)
    chosen = [
        (slot == jnp.where(offset == first + 2 * k, rank, -1.0)).astype(BF16)
        for k in range(len(pieces))
    ]
    return lax.dot_general(
        jnp.concatenate(chosen, axis=0),
        jnp.concatenate(pieces, axis=0),
        (((0,), (0,)), ((), ())),
        preferred_element_type=F32,
    )


def own_kernel(
    place, ids, cand, w0, w1, w2a, w2b, w3, f0, f1, f2, f3, part, rest, out_weight, rows_out
):
    width = cand.shape[1]
    values = cand[...].astype(F32)
    center = values - jnp.mean(values, axis=-1, keepdims=True)
    spread = jnp.mean(center * center, axis=-1, keepdims=True)
    normed = (center * lax.rsqrt(spread + 1e-06)).astype(BF16)
    rest[...] = dot(normed, natural_rows(place, 1, width)).astype(BF16)
    perm = natural_rows(place, 0, width)
    normed = dot(normed, perm).astype(BF16)
    shard = w0.shape[0]

    def weight(cols):
        parts = [(k * 5 + cols) * 16 for k in range(4)]
        own = [(ref, at) for ref in (w0, w1) for at in parts]
        own += [(w2a, parts[0]), (w2a, parts[1])]
        own += [(w2b, parts[2] - shard // 2), (w2b, parts[3] - shard // 2)]
        own += [(w3, at) for at in parts]
        return jnp.concatenate([ref[at : at + 16] for ref, at in own], axis=0)

    out_weight[...] = dot(perm, weight(4)).astype(BF16)
    for k in range(4):
        part[:, k * width : (k + 1) * width] = dot(normed, weight(k))
    rank, offset = row_keys(place, ids[...])
    total = place_rows(rank, offset, 0, [f0[:CAP], f1[:CAP], f2[:CAP], f3[:CAP]])
    total += place_rows(rank, offset, 1, [f0[CAP:], f1[CAP:], f2[CAP:], f3[CAP:]])
    rows_out[...] = total.astype(BF16)


def project_own(place, ids, cand, pieces, found):
    rows, width = cand.shape
    return pl.pallas_call(
        own_kernel,
        out_shape=(
            jax.ShapeDtypeStruct((rows, 4 * width), F32),
            jax.ShapeDtypeStruct((rows, width // 2), BF16),
            jax.ShapeDtypeStruct((width, width), BF16),
            jax.ShapeDtypeStruct((rows, width), BF16),
        ),
        in_specs=[pl.BlockSpec(memory_space=SMEM)] + [pl.BlockSpec(memory_space=VMEM)] * 11,
        out_specs=(pl.BlockSpec(memory_space=VMEM),) * 4,
        compiler_params=params(),
        name="project_own",
    )(place, ids, cand, *pieces, *found)


def rest_kernel(place, part, rest, own_weight, other, gate, query, self_term, out_weight):
    width = own_weight.shape[1]
    shard = other.shape[0] // 4
    normed = rest[...]

    def weight(cols):
        parts = [k * shard + (x * 5 + cols) * 16 for k in range(4) for x in range(4)]
        return jnp.concatenate([other[at : at + 16] for at in parts], axis=0)

    def proj(k):
        return silu(part[:, k * width : (k + 1) * width] + dot(normed, weight(k)))

    perm = natural_rows(place, 1, width)
    out_weight[...] = own_weight[...] + dot(perm, weight(4)).astype(BF16)
    gate[...] = proj(0)
    value = proj(1).astype(BF16).astype(F32)
    q = proj(2).astype(BF16)
    k = proj(3).astype(BF16)
    query[...] = q
    product = q.astype(F32) * k.astype(F32)
    head = width // HEADS
    for h in range(HEADS):
        cols = slice(h * head, (h + 1) * head)
        score = jnp.sum(product[:, cols], axis=-1, keepdims=True) * head ** (-0.5)
        self_term[:, cols] = silu(score).astype(BF16).astype(F32) * value[:, cols]


def project_rest(place, part, rest, own_weight, other):
    rows, width = part.shape[0], own_weight.shape[1]
    return pl.pallas_call(
        rest_kernel,
        out_shape=(
            jax.ShapeDtypeStruct((rows, width), F32),
            jax.ShapeDtypeStruct((rows, width), BF16),
            jax.ShapeDtypeStruct((rows, width), F32),
            jax.ShapeDtypeStruct((width, width), BF16),
        ),
        in_specs=[pl.BlockSpec(memory_space=SMEM)] + [pl.BlockSpec(memory_space=VMEM)] * 4,
        out_specs=(pl.BlockSpec(memory_space=VMEM),) * 4,
        compiler_params=params(),
        name="project",
        cost_estimate=pl.CostEstimate(flops=int(1.34e10), bytes_accessed=0, transcendentals=0),
    )(place, part, rest, own_weight, other)


def score_kernel(lengths, hist, query, self_term, gate, cand, out_weight, rows_ref, out):
    owners, users, per_owner, _ = hist.shape
    width = cand.shape[1]
    head = width // HEADS
    positions = owners * per_owner
    count = cand.shape[0] // users
    lane = iota((1, positions), 1)
    position = (lane % per_owner) * owners + lane // per_owner
    both = []
    for user in range(users):
        at = slice(user * count, (user + 1) * count)
        length = lengths[user]
        live = position < length
        kv = hist[:, user].reshape(positions, 2 * width)
        parts = []
        for h in range(HEADS):
            cols = slice(h * head, (h + 1) * head)
            scores = lax.dot_general(
                query[at, cols], kv[:, cols], (((1,), (1,)), ((), ())), preferred_element_type=F32
            ) * (head ** (-0.5))
            weights = jnp.where(live, silu(scores), 0.0).astype(BF16)
            parts.append(dot(weights, kv[:, width + h * head : width + (h + 1) * head]))
        attended = jnp.concatenate(parts, axis=1) + self_term[at]
        both.append(attended * (1.0 / (length.astype(F32) + 1.0)))
    attended = jnp.concatenate(both, axis=0)
    center = attended - jnp.mean(attended, axis=-1, keepdims=True)
    spread = jnp.mean(center * center, axis=-1, keepdims=True)
    gated = (center * gate[...] * lax.rsqrt(spread + 1e-06)).astype(BF16)
    final = cand[...].astype(F32) + dot(gated, out_weight[...])
    match = jnp.sum(final * rows_ref[...].astype(F32), axis=-1, keepdims=True)
    logit = match * lax.rsqrt(jnp.mean(final * final, axis=-1, keepdims=True) + 1e-06)
    eye = iota((count, count), 0) == iota((count, count), 1)
    for user in range(users):
        column = logit[user * count : (user + 1) * count]
        out[user : user + 1, :] = jnp.sum(jnp.where(eye, column, 0.0), axis=0, keepdims=True)


def score(lengths, hist, query, self_term, gate, cand, out_weight, rows):
    users = hist.shape[1]
    return pl.pallas_call(
        score_kernel,
        out_shape=jax.ShapeDtypeStruct((users, cand.shape[0] // users), F32),
        in_specs=[pl.BlockSpec(memory_space=SMEM)] + [pl.BlockSpec(memory_space=VMEM)] * 7,
        out_specs=pl.BlockSpec(memory_space=VMEM),
        compiler_params=params(),
        name="score",
    )(lengths, hist, query, self_term, gate, cand, out_weight, rows)


def along(axis, values, offset):
    size = lax.axis_size(axis)
    return lax.ppermute(values, axis, [(j, (j + offset) % size) for j in range(size)])


def swap_core(values):
    return lax.ppermute(values, "core", [(0, 1), (1, 0)])


def body(
    candidates, proj_weight, out_weight, history_kv, scorer_user, hist_len, cand_item, item_table
):
    users, count, width = candidates.shape
    cand = candidates.reshape(users * count, width)
    x, core = lax.axis_index("x"), lax.axis_index("core")
    item = x * 2 + core
    y, z = lax.axis_index("y"), lax.axis_index("z")
    place = jnp.stack([item, x, core, y, z]).astype(jnp.int32)
    owners = lax.axis_size(USER)

    hist = history_kv.reshape(history_kv.shape[0], history_kv.shape[1], -1)
    shard, picked = pick(scorer_user, place, proj_weight, out_weight, hist, owners, users)

    zs, items = lax.axis_size("z"), lax.axis_size(ITEM)
    shards = [
        lax.ppermute(
            shard,
            ("z",) + ITEM,
            [
                (k * items + i, (k + i + step) % zs * items + i)
                for k in range(zs)
                for i in range(items)
            ],
        )
        for step in (8, 0)
    ][::-1]

    arrived = lax.all_to_all(picked, USER, split_axis=0, concat_axis=0, tiled=True)

    my_ids = cand_item.reshape(1, users * count)

    blocked = block(*shards, my_ids)
    gathered = lax.all_gather(blocked, "x", axis=0, tiled=True)
    other_table = swap_core(later(blocked, item_table))
    weight = strip(gathered, other_table)
    half = weight.shape[0] // 2
    left, right = along("y", weight, 1), along("y", weight, 3)
    far_top, far_end = along("y", left[:half], 1), along("y", right[half:], 3)
    pieces = [weight, left, far_top, far_end, right]

    found = list(fetch(place, gathered, item_table, other_table))
    for k in (1, 3, 2):
        found[k] = along("x", found[k], k)
    other = swap_core(pack((0,) * 5, pieces, found[1:]))
    part, rest, own_weight, rows = project_own(place, my_ids, cand, pieces, found)
    gate, query, self_term, out_w = project_rest(place, part, rest, own_weight, other)
    return score(hist_len, arrived, query, self_term, gate, cand, out_w, rows)


def solution(mesh):
    cut = Mesh(mesh.devices.reshape(16, 4, 4, 2), ("z", "y", "x", "core"))
    return jax.shard_map(
        body,
        mesh=cut,
        in_specs=(
            P(USER + ITEM, None, None),
            P(USER, None),
            P(USER, None),
            P(ITEM, None, USER, None),
            P(),
            P(USER + ITEM),
            P(USER + ITEM, None),
            P(ITEM, None),
        ),
        out_specs=P(USER + ITEM, None),
        check_vma=False,
    )
```
